256 devices in a mesh: bucket: 32 (over z, y_hi, core), edge: 8 (over x, y_lo).
Axes of the slice: x: 4, y: 4 (y_hi: 2, y_lo: 2; y = y_hi * 2 + y_lo), z: 8, core: 2. Of those that a mesh axis runs over, the one named last changes fastest.
Arguments:
- left_slab: bfloat16 [49152, 256], P(('bucket', 'edge')), may hold values from -1.5 to 1.5
- right_slab: bfloat16 [49152, 256], P(('bucket', 'edge')), may hold values from -1.5 to 1.5
- relation: float32 [1024, 256], replicated, may hold values from 0.5 to 1.5
- src_ids: int32 [2, 32, 16384], P(None, 'bucket', 'edge'), may hold values from 0 to 1535
- dst_ids: int32 [2, 32, 16384], P(None, 'bucket', 'edge'), may hold values from 0 to 1535
- rel_ids: int32 [2, 32, 16384], P(None, 'bucket', 'edge'), may hold values from 0 to 1023
- neg_ids: int32 [2, 32, 64, 512], P(None, 'bucket', 'edge'), may hold values from 0 to 1535
- edge_counts: int32 [2, 32], P(None, 'bucket'), may hold values from 1 to 16384, as said below
Outputs:
- left_out: bfloat16 [49152, 256], P(('bucket', 'edge'))
- right_out: bfloat16 [49152, 256], P(('bucket', 'edge'))
- relation_out: float32 [1024, 256], replicated
The draws below stay inside these ranges and needn't reach their ends.
Inputs may be any that keep to these rules, and one draw needn't show every extreme that they name: `edge_counts`: live edges are the first slots of a bucket; in every round some bucket has all 16384 slots live.
All inputs are finite; a program needn't handle non-finite values.
Results may differ from the reference program's by a relative error of at most 0.0046.
Values may be sent and summed in bfloat16 or wider, within the bound.
No kernel may reach another device: no remote copies, remote signals or barrier semaphores. Data moves between devices by JAX's collectives and lax.ppermute only.
A program may use at most 64 MiB of HBM per device.

```python
import jax
import jax.numpy as jnp
from jax import lax

W = 256
RELS = 1024
SPAN = 256
NEG = 512
ROUNDS = 2
SPANS_DEV = 8
GROUPS = 32
SLAB = 1536
CAP = 16384
N_EDGE = 8


def draw_edge_counts(key, part):
    key_base = jax.random.fold_in(key, 11)
    key_full = jax.random.fold_in(key, 12)
    base = jax.random.randint(key_base, (ROUNDS, GROUPS), CAP // 8, CAP // 2 + 1)
    full = jax.random.randint(key_full, (ROUNDS,), 0, GROUPS)
    chosen = jnp.arange(GROUPS)[None, :] == full[:, None]
    return jnp.where(chosen, CAP, base).astype(jnp.int32)


def touch_ends(array, key, low, top_value):
    shape = array.shape
    index_at = [jax.random.randint(jax.random.fold_in(key, axis), (), 0, shape[axis]) for axis in range(len(shape))]
    array = array.at[tuple(index_at)].set(low)
    longest = shape.index(max(shape))
    index_at[longest] = (index_at[longest] + 1) % shape[longest]
    return array.at[tuple(index_at)].set(top_value)


def block_scale(rng, shape, cuts, smallest, high):
    loudness, own = 1.0, jax.random.fold_in(rng, 6)
    for axis_at, parts in cuts:
        draws = jnp.exp(jax.random.uniform(jax.random.fold_in(own, axis_at), (parts,), jnp.float32, smallest / len(cuts), high / len(cuts)))
        loudness = loudness * jnp.repeat(draws, shape[axis_at] // parts).reshape([-1 if axis == axis_at else 1 for axis in range(len(shape))])
    return loudness


def scatter_about(key, extent, width, most, pieces=(), kind=jnp.bfloat16):
    result = jax.random.normal(key, extent, jnp.float32) * width
    if len(pieces) > 0:
        result = block_scale(key, extent, pieces, -0.22, 0.18) * result
    return jnp.clip(result, min=-most, max=most).astype(kind)


def setup_inputs(seed: int = 0) -> dict:
    arg_keys = jax.random.split(jax.random.key(seed), 9)
    left_slab = scatter_about(arg_keys[0], (GROUPS * SLAB, W), 0.25, 1.5, ((0, 256),))
    right_slab = scatter_about(arg_keys[1], (GROUPS * SLAB, W), 0.25, 1.5, ((0, 256),))
    relation = jnp.clip(jax.random.uniform(arg_keys[2], (RELS, W), jnp.float32, 0.5, 1.5), 0.5, 1.5)
    src_ids = touch_ends(jax.random.randint(arg_keys[3], (ROUNDS, GROUPS, CAP), 0, SLAB), jax.random.fold_in(arg_keys[3], 1), 0, SLAB - 1).astype(jnp.int32)
    dst_ids = touch_ends(jax.random.randint(arg_keys[4], (ROUNDS, GROUPS, CAP), 0, SLAB), jax.random.fold_in(arg_keys[4], 1), 0, SLAB - 1).astype(jnp.int32)
    rel_ids = touch_ends(jax.random.randint(arg_keys[5], (ROUNDS, GROUPS, CAP), 0, RELS), jax.random.fold_in(arg_keys[5], 1), 0, RELS - 1).astype(jnp.int32)
    neg_ids = touch_ends(jax.random.randint(arg_keys[6], (ROUNDS, GROUPS, SPANS_DEV * N_EDGE, NEG), 0, SLAB), jax.random.fold_in(arg_keys[6], 1), 0, SLAB - 1).astype(jnp.int32)
    edge_counts = draw_edge_counts(jax.random.fold_in(arg_keys[8], 71), 0)
    return dict(left_slab=left_slab, right_slab=right_slab, relation=relation, src_ids=src_ids, dst_ids=dst_ids, rel_ids=rel_ids, neg_ids=neg_ids, edge_counts=edge_counts)


learn_rate = 0.05
relation_rate = 0.05


def span_grads(left, right, theta, src_c, dst_c, rel_c, neg_c, mask):
    s_rows = left[src_c]
    d_rows = right[dst_c]
    negatives = right[neg_c]
    t_rows = theta[rel_c]
    s_wide = s_rows.astype(jnp.float32)
    q_rows = (s_wide * t_rows).astype(jnp.bfloat16)
    q_wide = q_rows.astype(jnp.float32)
    d_wide = d_rows.astype(jnp.float32)
    pos = jnp.sum(q_wide * d_wide, axis=-1)
    scores = jnp.dot(q_rows, negatives.T, preferred_element_type=jnp.float32)
    g_pos = -jax.nn.sigmoid(-pos) * mask
    g_neg = (jax.nn.sigmoid(scores) * mask[:, None]).astype(jnp.bfloat16)
    g_q = g_pos[:, None] * d_wide + jnp.dot(g_neg, negatives, preferred_element_type=jnp.float32)
    g_d = g_pos[:, None] * q_wide
    g_negrows = jnp.dot(g_neg.T, q_rows, preferred_element_type=jnp.float32)
    g_s = g_q * t_rows
    g_t = g_q * s_wide
    return g_s, g_d, g_negrows, g_t


def bucket_grads(left, right, theta, src, dst, rel, neg, count):
    n_live = (count + SPAN - 1) // SPAN

    def step(c, carry):
        g_left, g_right, g_theta = carry
        mask = ((c * SPAN + jnp.arange(SPAN)) < count).astype(jnp.float32)
        g_s, g_d, g_negrows, g_t = span_grads(left, right, theta, src[c], dst[c], rel[c], neg[c], mask)
        g_left = g_left.at[src[c]].add(g_s)
        g_right = g_right.at[dst[c]].add(g_d).at[neg[c]].add(g_negrows)
        g_theta = g_theta.at[rel[c]].add(g_t)
        return g_left, g_right, g_theta

    init = (jnp.zeros((SLAB, W), jnp.float32), jnp.zeros((SLAB, W), jnp.float32), jnp.zeros((RELS, W), jnp.float32))
    return lax.fori_loop(0, n_live, step, init)


def reference(left_slab, right_slab, relation, src_ids, dst_ids, rel_ids, neg_ids, edge_counts):
    lefts = left_slab.reshape(GROUPS, SLAB, W)
    rights = right_slab.reshape(GROUPS, SLAB, W)
    theta = relation
    blocks = CAP // SPAN
    for rnd in range(ROUNDS):
        if rnd > 0:
            rights = jnp.roll(rights, 1, axis=0)
        src = src_ids[rnd].reshape(GROUPS, blocks, SPAN)
        dst = dst_ids[rnd].reshape(GROUPS, blocks, SPAN)
        rel = rel_ids[rnd].reshape(GROUPS, blocks, SPAN)
        neg = neg_ids[rnd]
        counts = edge_counts[rnd]

        def one_bucket(item):
            return bucket_grads(item[0], item[1], theta, item[2], item[3], item[4], item[5], item[6])

        g_left, g_right, g_theta = lax.map(one_bucket, (lefts, rights, src, dst, rel, neg, counts))
        lefts = (lefts.astype(jnp.float32) - learn_rate * g_left).astype(jnp.bfloat16)
        rights = (rights.astype(jnp.float32) - learn_rate * g_right).astype(jnp.bfloat16)
        theta = theta - relation_rate * jnp.sum(g_theta, axis=0)
    return lefts.reshape(GROUPS * SLAB, W), rights.reshape(GROUPS * SLAB, W), theta
```

```python
import jax
import jax.numpy as jnp
from jax import lax
from jax.experimental import pallas as pl
from jax.experimental.pallas import tpu as pltpu
from jax.sharding import PartitionSpec as P

ROUNDS = 2
GROUPS = 32
N_EDGE = 8
SLAB = 1536
RELS = 1024
W = 256
PIECE = SLAB // N_EDGE
CHUNK = 256

learn_rate = 0.05
relation_rate = 0.05

bf = jnp.bfloat16
f32 = jnp.float32


def dot(a, b):
    return jnp.dot(a, b, preferred_element_type=f32)


def dot_nt(a, b):
    return lax.dot_general(a, b, (((1,), (1,)), ((), ())), preferred_element_type=f32)


def count_kernel(neg_ref, out_ref):
    for b in range(neg_ref.shape[0]):
        ids = neg_ref[b : b + 1, :]
        negs = ids.shape[1]
        high = jnp.broadcast_to(ids >> 7, (16, negs)) == lax.broadcasted_iota(jnp.int32, (16, negs), 0)
        low = jnp.broadcast_to(ids & 127, (128, negs)) == lax.broadcasted_iota(jnp.int32, (128, negs), 0)
        table = dot_nt(jnp.where(high, 0.5, 0.0).astype(bf), jnp.where(low, 1.0, 0.0).astype(bf))
        for j in range(SLAB // 128):
            out_ref[b, 0:1, j * 128 : (j + 1) * 128] = table[j : j + 1, :]


def half_counts(neg):
    return pl.pallas_call(
        count_kernel, out_shape=jax.ShapeDtypeStruct((neg.shape[0], 1, SLAB), f32), name="half_counts"
    )(neg)


def grad_kernel(*refs):
    ids_ref, cnt_ref, hi_ref, lo_ref = refs[:4]
    left_in, right_in = refs[4:12], refs[12:20]
    left_out, right_out, theta_out = refs[20:28], refs[28:36], refs[36]
    left, right, acc_l, acc_r, acc_t = refs[37:]
    step = pl.program_id(0)

    @pl.when(step == 0)
    def _():
        for p in range(N_EDGE):
            left[p * PIECE : (p + 1) * PIECE, :] = left_in[p][...]
            right[p * PIECE : (p + 1) * PIECE, :] = right_in[p][...]
        acc_l[...] = jnp.zeros_like(acc_l)
        acc_r[...] = jnp.zeros_like(acc_r)
        acc_t[...] = jnp.zeros_like(acc_t)

    ids = ids_ref[0]
    edges = ids.shape[1]
    lane = lax.broadcasted_iota(jnp.int32, (edges, 128), 1)

    def column(k):
        return jnp.broadcast_to(ids[k : k + 1], (128, edges)).T

    def hits(col, j):
        return [col == lane + (j * CHUNK + 128 * h) for h in range(2)]

    def onehot(col, j):
        return jnp.concatenate([jnp.where(m, 1.0, 0.0).astype(bf) for m in hits(col, j)], axis=1)

    def rows(ref, j):
        return ref[j * CHUNK : (j + 1) * CHUNK, :]

    src, dst, rel = column(0), column(1), column(2)
    at_rel = [onehot(rel, j) for j in range(RELS // CHUNK)]
    at_src = [onehot(src, j) for j in range(SLAB // CHUNK)]
    t = sum(dot(at_rel[j], rows(hi_ref, j)) + dot(at_rel[j], rows(lo_ref, j)) for j in range(RELS // CHUNK))
    s = sum(dot(at_src[j], rows(left, j)) for j in range(SLAB // CHUNK))
    q = (s * t).astype(bf)
    q_half = q * bf(0.5)
    q_t = q.T
    gq = jnp.zeros((edges, W), f32)
    for j in range(SLAB // CHUNK):
        r = rows(right, j)
        tanh = jnp.tanh(dot_nt(q_half, r))
        count = cnt_ref[0, :, j * CHUNK : (j + 1) * CHUNK]
        g = []
        for h, m in enumerate(hits(dst, j)):
            c = count[:, h * 128 : (h + 1) * 128]
            g.append((jnp.where(m, c + 0.5, c) * tanh[:, h * 128 : (h + 1) * 128] + jnp.where(m, c - 0.5, c)).astype(bf))
        g = jnp.concatenate(g, axis=1)
        gq += dot(g, r)
        acc_r[:, j * CHUNK : (j + 1) * CHUNK] += dot(q_t, g)
    gs = (gq * t).astype(bf).T
    gt = (gq * s).astype(bf).T
    for j in range(SLAB // CHUNK):
        acc_l[:, j * CHUNK : (j + 1) * CHUNK] += dot(gs, at_src[j])
    for j in range(RELS // CHUNK):
        acc_t[:, j * CHUNK : (j + 1) * CHUNK] += dot(gt, at_rel[j])

    @pl.when(step == pl.num_programs(0) - 1)
    def _():
        for acc, outs in ((acc_l, left_out), (acc_r, right_out)):
            for j in range(SLAB // CHUNK):
                block = acc[:, j * CHUNK : (j + 1) * CHUNK].T
                for m in range(0, CHUNK, 64):
                    p, off = divmod(j * CHUNK + m, PIECE)
                    outs[p][off : off + 64, :] = block[m : m + 64, :].astype(outs[p].dtype)
        for j in range(RELS // CHUNK):
            theta_out[j * CHUNK : (j + 1) * CHUNK, :] = acc_t[:, j * CHUNK : (j + 1) * CHUNK].T.astype(bf)


def bucket_grads(ids, counts, theta, lefts, rights):
    hi = theta.astype(bf)
    lo = (theta - hi.astype(f32)).astype(bf)
    whole = lambda a: pl.BlockSpec(a.shape, lambda i: (0,) * len(a.shape))
    one = lambda a: pl.BlockSpec((1,) + a.shape[1:], lambda i: (i, 0, 0))
    pieces = [jax.ShapeDtypeStruct((PIECE, W), f32 if p == 0 else bf) for p in range(N_EDGE)]
    outs = pieces + pieces + [jax.ShapeDtypeStruct((RELS, W), bf)]
    got = pl.pallas_call(
        grad_kernel,
        grid=(ids.shape[0],),
        in_specs=[one(ids), one(counts), whole(hi), whole(lo)] + [whole(a) for a in lefts + rights],
        out_specs=[whole(a) for a in outs],
        out_shape=outs,
        scratch_shapes=[
            pltpu.VMEM((SLAB, W), bf),
            pltpu.VMEM((SLAB, W), bf),
            pltpu.VMEM((W, SLAB), f32),
            pltpu.VMEM((W, SLAB), f32),
            pltpu.VMEM((W, RELS), f32),
        ],
        compiler_params=pltpu.CompilerParams(vmem_limit_bytes=48 << 20),
        name="bucket_grads",
    )(ids, counts, hi, lo, *lefts, *rights)
    return got[:N_EDGE], got[N_EDGE : 2 * N_EDGE], got[2 * N_EDGE]


def shift(x, k):
    return lax.ppermute(x, "edge", [(i, (i + k) % N_EDGE) for i in range(N_EDGE)])


def shift_both(x, k):
    route = [
        (b * N_EDGE + e, (b + 1) % GROUPS * N_EDGE + (e + k) % N_EDGE) for b in range(GROUPS) for e in range(N_EDGE)
    ]
    return lax.ppermute(x, ("bucket", "edge"), route)


def gathered(x):
    return [x] + [shift(x, p) for p in range(1, N_EDGE)]


def scattered_sum(pieces):
    total = pieces[0]
    for p in range(1, N_EDGE):
        total = total + shift(pieces[p], -p).astype(f32)
    return total


def exchange(x, axis):
    return lax.all_to_all(x, axis, 0, 0)


def theta_sum(g):
    mine = jnp.sum(exchange(g.reshape(N_EDGE, RELS // N_EDGE, W), "edge").astype(f32), 0)
    few = jnp.sum(exchange(mine.astype(bf).reshape(GROUPS, -1, W), "bucket").astype(f32), 0).astype(bf)
    rows = exchange(jnp.broadcast_to(few[None], (GROUPS,) + few.shape), "bucket").reshape(-1, W)
    return exchange(jnp.broadcast_to(rows[None], (N_EDGE,) + rows.shape), "edge").reshape(RELS, W).astype(f32)


def descend(slab, grad):
    return (slab.astype(f32) - learn_rate * grad).astype(bf)


def body(left_slab, right_slab, relation, src_ids, dst_ids, rel_ids, neg_ids, edge_counts):
    me = lax.axis_index("edge")
    blocks = neg_ids.shape[2]
    width = src_ids.shape[2] // blocks

    def local(ids):
        owner = ids // PIECE
        return lax.rem(me - owner + N_EDGE, N_EDGE) * PIECE + (ids - owner * PIECE)

    lefts = gathered(left_slab)
    rights = gathered(right_slab)
    slot = me * blocks * width + jnp.arange(blocks * width)
    live = slot[None] < edge_counts
    src = jnp.where(live, local(src_ids[:, 0]), -1)
    rel = jnp.where(live, rel_ids[:, 0], -1)
    dst = local(dst_ids[:, 0])
    ids = jnp.stack([a.reshape(ROUNDS, blocks, width) for a in (src, dst, rel)] + [jnp.zeros((ROUNDS, blocks, width), jnp.int32)] * 5, 2)
    counts = half_counts(local(neg_ids[:, 0]).reshape(ROUNDS * blocks, -1)).reshape(ROUNDS, blocks, 1, SLAB)
    theta = relation
    for rnd in range(ROUNDS):
        g_left, g_right, g_theta = bucket_grads(ids[rnd], counts[rnd], theta, lefts, rights)
        left = descend(lefts[0], scattered_sum(g_left))
        right = descend(rights[0], scattered_sum(g_right))
        theta = theta - relation_rate * theta_sum(g_theta)
        if rnd + 1 < ROUNDS:
            lefts = gathered(left)
            rights = [shift_both(right, p) for p in range(N_EDGE)]
    return (left, right, theta)


def solution(mesh):
    placed = (
        P(("bucket", "edge"), None),
        P(("bucket", "edge"), None),
        P(),
        P(None, "bucket", "edge"),
        P(None, "bucket", "edge"),
        P(None, "bucket", "edge"),
        P(None, "bucket", "edge", None),
        P(None, "bucket"),
    )
    return jax.shard_map(
        body,
        mesh=mesh,
        in_specs=placed,
        out_specs=(P(("bucket", "edge"), None), P(("bucket", "edge"), None), P()),
        check_vma=False,
    )
```

```python
import jax
import jax.numpy as jnp
from jax import lax
from jax.experimental import pallas as pl
from jax.experimental.pallas import tpu as pltpu
from jax.sharding import Mesh
from jax.sharding import PartitionSpec as P

ROUNDS = 2
N_EDGE = 8
SLAB = 1536
RELS = 1024
W = 256
BOTH = 2 * (SLAB // N_EDGE)
PIECE = SLAB // N_EDGE
SHARE = 32
CHUNK = 256
SPAN = 256

learn_rate = 0.05
relation_rate = 0.05

EDGE = ("x", "y_lo")
BUCKET = ("z", "y_hi", "core")
PLANE = EDGE + ("y_hi", "core")

bf = jnp.bfloat16
f32 = jnp.float32


def dot(a, b):
    return jnp.dot(a, b, preferred_element_type=f32)


def dot_nt(a, b):
    return lax.dot_general(a, b, (((1,), (1,)), ((), ())), preferred_element_type=f32)


def count_kernel(neg_ref, out_ref):
    for b in range(neg_ref.shape[0]):
        ids = neg_ref[b : b + 1, :]
        negs = ids.shape[1]
        high = jnp.broadcast_to(ids >> 7, (16, negs)) == lax.broadcasted_iota(jnp.int32, (16, negs), 0)
        low = jnp.broadcast_to(ids & 127, (128, negs)) == lax.broadcasted_iota(jnp.int32, (128, negs), 0)
        table = dot_nt(jnp.where(high, 0.5, 0.0).astype(bf), jnp.where(low, 1.0, 0.0).astype(bf))
        for j in range(SLAB // 128):
            out_ref[b, 0:1, j * 128 : (j + 1) * 128] = table[j : j + 1, :]


def half_counts(neg):
    return pl.pallas_call(
        count_kernel, out_shape=jax.ShapeDtypeStruct((neg.shape[0], 1, SLAB), f32), name="half_counts"
    )(neg)


def params(mib):
    return pltpu.CompilerParams(vmem_limit_bytes=mib << 20)


def whole(a):
    return pl.BlockSpec(a.shape, lambda *_: (0,) * len(a.shape))


def shape(dims, dtype):
    return jax.ShapeDtypeStruct(dims, dtype)


def columns(ids_ref, k):
    ids = [ids_ref[b, k : k + 1, :] for b in range(ids_ref.shape[0])]
    return jnp.concatenate([jnp.broadcast_to(a, (128, a.shape[1])).T for a in ids])


def hits(col, j):
    lane = lax.broadcasted_iota(jnp.int32, col.shape, 1)
    return [col == lane + (j * CHUNK + 128 * h) for h in range(2)]


def onehot(col, j):
    col = col.astype(jnp.int16)
    lane = lax.broadcasted_iota(jnp.int16, col.shape, 1)
    one, zero = jnp.ones(col.shape, bf), jnp.zeros(col.shape, bf)
    return jnp.concatenate([jnp.where(col == lane + jnp.int16(j * CHUNK + 128 * h), one, zero) for h in range(2)], axis=1)


def rows(ref, j):
    return ref[j * CHUNK : (j + 1) * CHUNK, :]


def relation_kernel(ids_ref, theta_ref, step_ref, t_ref, halves):
    @pl.when(pl.program_id(0) == 0)
    def _():
        theta = theta_ref[...] - relation_rate * step_ref[...].astype(f32)
        halves[:RELS, :] = theta.astype(bf)
        halves[RELS:, :] = (theta - theta.astype(bf).astype(f32)).astype(bf)

    rel = columns(ids_ref, 2)
    at_rel = jnp.concatenate([onehot(rel, j) for j in range(RELS // CHUNK)] * 2, axis=1)
    t_ref[...] = dot(at_rel, halves[...])


def relation_rows(ids, theta, theta_step):
    blocks, _, width = ids.shape
    return pl.pallas_call(
        relation_kernel,
        grid=(blocks // 4,),
        in_specs=[pl.BlockSpec((4,) + ids.shape[1:], lambda i: (i, 0, 0)), whole(theta), whole(theta_step)],
        out_specs=pl.BlockSpec((4 * width, W), lambda i: (i, 0)),
        out_shape=shape((blocks * width, W), f32),
        scratch_shapes=[pltpu.VMEM((2 * RELS, W), bf)],
        compiler_params=params(8),
        cost_estimate=pl.CostEstimate(flops=4_000_000_000, bytes_accessed=4_000_000, transcendentals=0),
        name="relation_rows",
    )(ids, theta, theta_step)


def grad_kernel(ids_ref, cnt_ref, t_ref, *refs):
    slabs, slab_out, theta_out = refs[:N_EDGE], refs[N_EDGE : 2 * N_EDGE], refs[2 * N_EDGE]
    left, right, all_src, all_g, all_rel, all_q, all_gs, all_gt = refs[2 * N_EDGE + 1 :]
    step = pl.program_id(0)

    @pl.when(step == 0)
    def _():
        for p in range(N_EDGE):
            left[p * PIECE : (p + 1) * PIECE, :] = slabs[p][:PIECE, :]
            right[p * PIECE : (p + 1) * PIECE, :] = slabs[p][PIECE:, :]


    src, dst, rel = (columns(ids_ref, k) for k in range(3))
    at_src = jnp.concatenate([onehot(src, j) for j in range(SLAB // CHUNK)], axis=1)
    at_rel = jnp.concatenate([onehot(rel, j) for j in range(RELS // CHUNK)], axis=1)
    t = t_ref[...]
    s = dot(at_src, left[...])
    q = (s * t).astype(bf)
    tanh = jnp.tanh(dot_nt(q * bf(0.5), right[...]))
    g = []
    for j in range(SLAB // CHUNK):
        for h, m in enumerate(hits(dst, j)):
            at = j * CHUNK + h * 128
            part = []
            for b in range(cnt_ref.shape[0]):
                e = slice(b * SPAN, (b + 1) * SPAN)
                c = cnt_ref[b, :, at : at + 128]
                part.append((jnp.where(m[e], c + 0.5, c) * tanh[e, at : at + 128] + jnp.where(m[e], c - 0.5, c)).astype(bf))
            g.append(jnp.concatenate(part))
    g = jnp.concatenate(g, axis=1)
    gq = dot(g, right[...])
    q_t = q.T
    gs = (gq * t).astype(bf).T
    gt = (gq * s).astype(bf).T
    e = pl.ds(pl.multiple_of(step * 1024, 1024), 1024)
    all_src[e, :] = at_src
    all_g[e, :] = g
    all_rel[e, :] = at_rel
    all_q[:, e] = q_t
    all_gs[:, e] = gs
    all_gt[:, e] = gt

    @pl.when(step == pl.num_programs(0) - 1)
    def _():
        for first, get in ((0, lambda j: dot(all_gs[...], all_src[:, j * CHUNK : (j + 1) * CHUNK])), (PIECE, lambda j: dot(all_q[...], all_g[:, j * CHUNK : (j + 1) * CHUNK]))):
            for j in range(SLAB // CHUNK):
                block = get(j).T.astype(bf)
                for m in range(0, CHUNK, 64):
                    p, off = divmod(j * CHUNK + m, PIECE)
                    slab_out[p][first + off : first + off + 64, :] = block[m : m + 64, :]
        for j in range(RELS // CHUNK):
            block = dot(all_gt[...], all_rel[:, j * CHUNK : (j + 1) * CHUNK]).T.astype(bf)
            for m in range(0, CHUNK, SHARE):
                theta_out[(j * CHUNK + m) // SHARE] = block[m : m + SHARE, :]


def bucket_grads(ids, counts, t, slabs):
    blocks, _, width = ids.shape
    one = lambda a: pl.BlockSpec((4,) + a.shape[1:], lambda i: (i, 0, 0))
    outs = [shape((BOTH, W), bf)] * N_EDGE + [shape((RELS // SHARE, SHARE, W), bf)]
    *g_slabs, g_theta = pl.pallas_call(
        grad_kernel,
        grid=(blocks // 4,),
        in_specs=[one(ids), one(counts), pl.BlockSpec((4 * width, W), lambda i: (i, 0))] + [whole(a) for a in slabs],
        out_specs=[whole(a) for a in outs],
        out_shape=outs,
        scratch_shapes=[
            pltpu.VMEM((SLAB, W), bf),
            pltpu.VMEM((SLAB, W), bf),
            pltpu.VMEM((2048, SLAB), bf),
            pltpu.VMEM((2048, SLAB), bf),
            pltpu.VMEM((2048, RELS), bf),
            pltpu.VMEM((W, 2048), bf),
            pltpu.VMEM((W, 2048), bf),
            pltpu.VMEM((W, 2048), bf),
        ],
        compiler_params=params(36),
        cost_estimate=pl.CostEstimate(flops=18_000_000_000, bytes_accessed=8_000_000, transcendentals=0),
        name="bucket_grads",
    )(ids, counts, t, *slabs)
    return g_slabs, g_theta


def summed(x):
    total = x[0].astype(f32)
    for k in range(1, x.shape[0]):
        total = total + x[k].astype(f32)
    return total.astype(bf)


def descend_kernel(old_ref, *refs):
    parts, left_ref, right_ref = refs[:N_EDGE], refs[N_EDGE], refs[N_EDGE + 1]
    total = parts[0][...].astype(f32)
    for part in parts[1:]:
        total = total + part[...].astype(f32)
    new = (old_ref[...].astype(f32) - learn_rate * total).astype(bf)
    left_ref[...] = new[:PIECE]
    right_ref[...] = new[PIECE:]


def descend(parts, old):
    out = shape((PIECE, W), bf)
    return pl.pallas_call(descend_kernel, out_shape=[out, out], name="descend")(old, *parts)


def exchange(x, axes):
    return lax.all_to_all(x, axes, 0, 0)


def to_all(x, axes):
    n = lax.axis_size(axes)
    return exchange(jnp.broadcast_to(x[None], (n,) + x.shape), axes)


def along_edge(x, k):
    n = lax.axis_size(EDGE)
    return lax.ppermute(x, EDGE, [(i, (i + k) % n) for i in range(n)])


def gathered(x):
    return [x] + [along_edge(x, p) for p in range(1, N_EDGE)]


def returned(pieces):
    return [pieces[0]] + [along_edge(pieces[p], -p) for p in range(1, N_EDGE)]


def next_group(x):
    n = lax.axis_size(BUCKET)
    return lax.ppermute(x, BUCKET, [(i, (i + 1) % n) for i in range(n)])


def theta_sum(g):
    g = summed(exchange(g, PLANE))
    g = summed(to_all(g, "z"))
    return to_all(g, PLANE).reshape(RELS, W)


def body(left_slab, right_slab, relation, src_ids, dst_ids, rel_ids, neg_ids, edge_counts):
    me = lax.axis_index(EDGE)
    blocks = neg_ids.shape[2]
    width = src_ids.shape[2] // blocks

    def local(ids):
        owner = ids // PIECE
        return lax.rem(me - owner + N_EDGE, N_EDGE) * PIECE + (ids - owner * PIECE)

    own = jnp.concatenate([left_slab, right_slab])
    slabs = gathered(own)
    slot = me * blocks * width + jnp.arange(blocks * width)
    live = slot[None] < edge_counts
    src = jnp.where(live, local(src_ids[:, 0]), -1)
    rel = jnp.where(live, rel_ids[:, 0], -1)
    ids = jnp.stack([a.reshape(ROUNDS, blocks, width) for a in (src, local(dst_ids[:, 0]), rel)] + [jnp.zeros((ROUNDS, blocks, width), jnp.int32)] * 5, 2)
    counts = half_counts(local(neg_ids[:, 0]).reshape(ROUNDS * blocks, -1)).reshape(ROUNDS, blocks, 1, SLAB)
    theta = relation
    theta_step = jnp.zeros((RELS, W), bf)
    for rnd in range(ROUNDS):
        t = relation_rows(ids[rnd], theta, theta_step)
        g_slabs, g_theta = bucket_grads(ids[rnd], counts[rnd], t, slabs)
        if rnd > 0:
            theta = theta - relation_rate * theta_step.astype(f32)
        theta_step = theta_sum(g_theta)
        left, right = descend(returned(g_slabs), own)
        if rnd + 1 < ROUNDS:
            own = jnp.concatenate([left, next_group(right)])
            slabs = gathered(own)
    return (left, right, theta - relation_rate * theta_step.astype(f32))


def solution(mesh):
    fine = Mesh(mesh.devices.reshape(8, 2, 2, 4, 2), BUCKET + EDGE)
    rows = P(BUCKET + EDGE, None)
    placed = (
        rows,
        rows,
        P(),
        P(None, BUCKET, EDGE),
        P(None, BUCKET, EDGE),
        P(None, BUCKET, EDGE),
        P(None, BUCKET, EDGE, None),
        P(None, BUCKET),
    )
    return jax.shard_map(
        body,
        mesh=fine,
        in_specs=placed,
        out_specs=(rows, rows, P()),
        check_vma=False,
    )
```

```python
import jax
import jax.numpy as jnp
from jax import lax
from jax.experimental import pallas as pl
from jax.experimental.pallas import tpu as pltpu
from jax.sharding import Mesh
from jax.sharding import PartitionSpec as P

ROUNDS = 2
N_EDGE = 8
SLAB = 1536
RELS = 1024
W = 256
BOTH = 2 * (SLAB // N_EDGE)
PIECE = SLAB // N_EDGE
SHARE = 32
CHUNK = 256
SPAN = 256

learn_rate = 0.05
relation_rate = 0.05

EDGE = ("x", "y_lo")
BUCKET = ("z", "y_hi", "core")
PLANE = EDGE + ("y_hi", "core")

bf = jnp.bfloat16
f32 = jnp.float32


def dot(a, b):
    return jnp.dot(a, b, preferred_element_type=f32)


def dot_nt(a, b):
    return lax.dot_general(a, b, (((1,), (1,)), ((), ())), preferred_element_type=f32)


def params(mib):
    return pltpu.CompilerParams(vmem_limit_bytes=mib << 20)


def count_kernel(neg_ref, out_ref):
    for b in range(neg_ref.shape[0]):
        ids = neg_ref[b : b + 1, :]
        negs = ids.shape[1]
        high = jnp.broadcast_to(ids >> 7, (16, negs)) == lax.broadcasted_iota(jnp.int32, (16, negs), 0)
        low = jnp.broadcast_to(ids & 127, (128, negs)) == lax.broadcasted_iota(jnp.int32, (128, negs), 0)
        table = dot_nt(jnp.where(high, 0.5, 0.0).astype(bf), jnp.where(low, 1.0, 0.0).astype(bf))
        for j in range(SLAB // 128):
            out_ref[b, 0:1, j * 128 : (j + 1) * 128] = table[j : j + 1, :]


def half_counts(neg):
    return pl.pallas_call(
        count_kernel, out_shape=jax.ShapeDtypeStruct((neg.shape[0], 1, SLAB), f32), compiler_params=params(36), name="half_counts"
    )(neg)


def whole(a):
    return pl.BlockSpec(a.shape, lambda *_: (0,) * len(a.shape))


def shape(dims, dtype):
    return jax.ShapeDtypeStruct(dims, dtype)


def columns(ids_ref, k):
    ids = [ids_ref[b, k : k + 1, :] for b in range(ids_ref.shape[0])]
    return jnp.concatenate([jnp.broadcast_to(a, (128, a.shape[1])).T for a in ids])


def hits(col, j):
    lane = lax.broadcasted_iota(jnp.int32, col.shape, 1)
    return [col == lane + (j * CHUNK + 128 * h) for h in range(2)]


def onehot(col, j):
    col = col.astype(jnp.int16)
    lane = lax.broadcasted_iota(jnp.int16, col.shape, 1)
    one, zero = jnp.ones(col.shape, bf), jnp.zeros(col.shape, bf)
    return jnp.concatenate([jnp.where(col == lane + jnp.int16(j * CHUNK + 128 * h), one, zero) for h in range(2)], axis=1)


def rows(ref, j):
    return ref[j * CHUNK : (j + 1) * CHUNK, :]


def relation_kernel(ids_ref, theta_ref, step_ref, t_ref, halves):
    @pl.when(pl.program_id(0) == 0)
    def _():
        theta = theta_ref[...] - relation_rate * step_ref[...].astype(f32)
        halves[:RELS, :] = theta.astype(bf)
        halves[RELS:, :] = (theta - theta.astype(bf).astype(f32)).astype(bf)

    rel = columns(ids_ref, 2)
    at_rel = jnp.concatenate([onehot(rel, j) for j in range(RELS // CHUNK)] * 2, axis=1)
    t_ref[...] = dot(at_rel, halves[...])


def relation_rows(ids, theta, theta_step):
    blocks, _, width = ids.shape
    return pl.pallas_call(
        relation_kernel,
        grid=(blocks // 4,),
        in_specs=[pl.BlockSpec((4,) + ids.shape[1:], lambda i: (i, 0, 0)), whole(theta), whole(theta_step)],
        out_specs=pl.BlockSpec((4 * width, W), lambda i: (i, 0)),
        out_shape=shape((blocks * width, W), f32),
        scratch_shapes=[pltpu.VMEM((2 * RELS, W), bf)],
        compiler_params=params(36),
        cost_estimate=pl.CostEstimate(flops=20_000_000_000, bytes_accessed=4_000_000, transcendentals=0),
        name="relation_rows",
    )(ids, theta, theta_step)


def grad_kernel(ids_ref, cnt_ref, t_ref, *refs):
    slabs, slab_out, theta_out = refs[:N_EDGE], refs[N_EDGE : 2 * N_EDGE], refs[2 * N_EDGE]
    left, right, all_src, all_g, all_rel, all_q, all_gs, all_gt, sems = refs[2 * N_EDGE + 1 :]
    step = pl.program_id(0)

    @pl.when(step == 0)
    def _():
        copies = []
        for p in range(N_EDGE):
            own = pl.ds(p * PIECE, PIECE)
            copies.append(pltpu.make_async_copy(slabs[p].at[pl.ds(0, PIECE)], left.at[own], sems.at[2 * p]))
            copies.append(pltpu.make_async_copy(slabs[p].at[pl.ds(PIECE, PIECE)], right.at[own], sems.at[2 * p + 1]))
        for copy in copies:
            copy.start()
        for copy in copies:
            copy.wait()


    src, dst, rel = (columns(ids_ref, k) for k in range(3))
    at_src = jnp.concatenate([onehot(src, j) for j in range(SLAB // CHUNK)], axis=1)
    at_rel = jnp.concatenate([onehot(rel, j) for j in range(RELS // CHUNK)], axis=1)
    t = t_ref[...]
    s = dot(at_src, left[...])
    q = (s * t).astype(bf)
    tanh = jnp.tanh(dot_nt(q * bf(0.5), right[...]))
    g = []
    for j in range(SLAB // CHUNK):
        for h, m in enumerate(hits(dst, j)):
            at = j * CHUNK + h * 128
            part = []
            for b in range(cnt_ref.shape[0]):
                e = slice(b * SPAN, (b + 1) * SPAN)
                c = cnt_ref[b, :, at : at + 128]
                part.append((jnp.where(m[e], c + 0.5, c) * tanh[e, at : at + 128] + jnp.where(m[e], c - 0.5, c)).astype(bf))
            g.append(jnp.concatenate(part))
    g = jnp.concatenate(g, axis=1)
    gq = dot(g, right[...])
    q_t = q.T
    gs = (gq * t).astype(bf).T
    gt = (gq * s).astype(bf).T
    e = pl.ds(pl.multiple_of(step * 1024, 1024), 1024)
    all_src[e, :] = at_src
    all_g[e, :] = g
    all_rel[e, :] = at_rel
    all_q[:, e] = q_t
    all_gs[:, e] = gs
    all_gt[:, e] = gt

    @pl.when(step == pl.num_programs(0) - 1)
    def _():
        for first, get in ((0, lambda j: dot(all_gs[...], all_src[:, j * CHUNK : (j + 1) * CHUNK])), (PIECE, lambda j: dot(all_q[...], all_g[:, j * CHUNK : (j + 1) * CHUNK]))):
            for j in range(SLAB // CHUNK):
                block = get(j).T.astype(bf)
                for m in range(0, CHUNK, 64):
                    p, off = divmod(j * CHUNK + m, PIECE)
                    slab_out[p][first + off : first + off + 64, :] = block[m : m + 64, :]
        for j in range(RELS // CHUNK):
            block = dot(all_gt[...], all_rel[:, j * CHUNK : (j + 1) * CHUNK]).T.astype(bf)
            for m in range(0, CHUNK, SHARE):
                theta_out[(j * CHUNK + m) // SHARE] = block[m : m + SHARE, :]


def bucket_grads(ids, counts, t, slabs):
    blocks, _, width = ids.shape
    one = lambda a: pl.BlockSpec((4,) + a.shape[1:], lambda i: (i, 0, 0))
    outs = [shape((BOTH, W), bf)] * N_EDGE + [shape((RELS // SHARE, SHARE, W), bf)]
    *g_slabs, g_theta = pl.pallas_call(
        grad_kernel,
        grid=(blocks // 4,),
        in_specs=[one(ids), one(counts), pl.BlockSpec((4 * width, W), lambda i: (i, 0))] + [pl.BlockSpec(memory_space=pltpu.HBM)] * N_EDGE,
        out_specs=[whole(a) for a in outs],
        out_shape=outs,
        scratch_shapes=[
            pltpu.VMEM((SLAB, W), bf),
            pltpu.VMEM((SLAB, W), bf),
            pltpu.VMEM((2048, SLAB), bf),
            pltpu.VMEM((2048, SLAB), bf),
            pltpu.VMEM((2048, RELS), bf),
            pltpu.VMEM((W, 2048), bf),
            pltpu.VMEM((W, 2048), bf),
            pltpu.VMEM((W, 2048), bf),
            pltpu.SemaphoreType.DMA((2 * N_EDGE,)),
        ],
        compiler_params=params(36),
        cost_estimate=pl.CostEstimate(flops=18_000_000_000, bytes_accessed=8_000_000, transcendentals=0),
        name="bucket_grads",
    )(ids, counts, t, *slabs)
    return g_slabs, g_theta


def summed(x):
    total = x[0].astype(f32)
    for k in range(1, x.shape[0]):
        total = total + x[k].astype(f32)
    return total.astype(bf)


def descend_kernel(old_ref, *refs):
    parts, left_ref, right_ref = refs[:N_EDGE], refs[N_EDGE], refs[N_EDGE + 1]
    total = parts[0][...].astype(f32)
    for part in parts[1:]:
        total = total + part[...].astype(f32)
    new = (old_ref[...].astype(f32) - learn_rate * total).astype(bf)
    left_ref[...] = new[:PIECE]
    right_ref[...] = new[PIECE:]


def descend(parts, old):
    out = shape((PIECE, W), bf)
    return pl.pallas_call(descend_kernel, out_shape=[out, out], compiler_params=params(36), name="descend")(old, *parts)


def exchange(x, axes):
    return lax.all_to_all(x, axes, 0, 0)


def to_all(x, axes):
    n = lax.axis_size(axes)
    return exchange(jnp.broadcast_to(x[None], (n,) + x.shape), axes)


def along_edge(x, k):
    n = lax.axis_size(EDGE)
    return lax.ppermute(x, EDGE, [(i, (i + k) % n) for i in range(n)])


def gathered(x):
    return [x] + [along_edge(x, p) for p in range(1, N_EDGE)]


def returned(pieces):
    return [pieces[0]] + [along_edge(pieces[p], -p) for p in range(1, N_EDGE)]


def next_group(x):
    n = lax.axis_size(BUCKET)
    return lax.ppermute(x, BUCKET, [(i, (i + 1) % n) for i in range(n)])


def body(left_slab, right_slab, relation, src_ids, dst_ids, rel_ids, neg_ids, edge_counts):
    me = lax.axis_index(EDGE)
    blocks = neg_ids.shape[2]
    width = src_ids.shape[2] // blocks

    def local(ids):
        owner = ids // PIECE
        return lax.rem(me - owner + N_EDGE, N_EDGE) * PIECE + (ids - owner * PIECE)

    own = jnp.concatenate([left_slab, right_slab])
    slabs = gathered(own)
    slot = me * blocks * width + jnp.arange(blocks * width)
    live = slot[None] < edge_counts
    src = jnp.where(live, local(src_ids[:, 0]), -1)
    rel = jnp.where(live, rel_ids[:, 0], -1)
    ids = jnp.stack([a.reshape(ROUNDS, blocks, width) for a in (src, local(dst_ids[:, 0]), rel)] + [jnp.zeros((ROUNDS, blocks, width), jnp.int32)] * 5, 2)
    counts = half_counts(local(neg_ids[:, 0]).reshape(ROUNDS * blocks, -1)).reshape(ROUNDS, blocks, 1, SLAB)
    theta = relation
    theta_step = jnp.zeros((RELS, W), bf)
    for rnd in range(ROUNDS):
        t = relation_rows(ids[rnd], theta, theta_step)
        g_slabs, g_theta = bucket_grads(ids[rnd], counts[rnd], t, slabs)
        if rnd > 0:
            theta = theta - relation_rate * theta_step.astype(f32)
        parts = returned(g_slabs)
        g_theta = summed(to_all(summed(exchange(g_theta, PLANE)), "z"))
        if rnd + 1 == ROUNDS:
            parts, g_theta = lax.optimization_barrier((parts, g_theta))
        theta_step = to_all(g_theta, PLANE).reshape(RELS, W)
        left, right = descend(parts, own)
        if rnd + 1 < ROUNDS:
            own = jnp.concatenate([left, next_group(right)])
            slabs = gathered(own)
    return (left, right, theta - relation_rate * theta_step.astype(f32))


def solution(mesh):
    fine = Mesh(mesh.devices.reshape(8, 2, 2, 4, 2), BUCKET + EDGE)
    rows = P(BUCKET + EDGE, None)
    placed = (
        rows,
        rows,
        P(),
        P(None, BUCKET, EDGE),
        P(None, BUCKET, EDGE),
        P(None, BUCKET, EDGE),
        P(None, BUCKET, EDGE, None),
        P(None, BUCKET),
    )
    return jax.shard_map(
        body,
        mesh=fine,
        in_specs=placed,
        out_specs=(rows, rows, P()),
        check_vma=False,
    )
```

```python
import jax
import jax.numpy as jnp
from jax import lax
from jax.experimental import pallas as pl
from jax.experimental.pallas import tpu as pltpu
from jax.sharding import Mesh
from jax.sharding import PartitionSpec as P

ROUNDS = 2
N_EDGE = 8
SLAB = 1536
RELS = 1024
W = 256
BOTH = 2 * (SLAB // N_EDGE)
PIECE = SLAB // N_EDGE
SHARE = 32
SHIFTS = (4, 3, 5, 2, 6, 7, 1)
CHUNK = 256
SPAN = 256

learn_rate = 0.05
relation_rate = 0.05

EDGE = ("x", "y_lo")
BUCKET = ("z", "y_hi", "core")
PLANE = EDGE + ("y_hi", "core")

bf = jnp.bfloat16
f32 = jnp.float32


def dot(a, b):
    return jnp.dot(a, b, preferred_element_type=f32)


def dot_nt(a, b):
    return lax.dot_general(a, b, (((1,), (1,)), ((), ())), preferred_element_type=f32)


def params(mib):
    return pltpu.CompilerParams(vmem_limit_bytes=mib << 20)


def count_kernel(neg_ref, out_ref):
    for b in range(neg_ref.shape[0]):
        ids = neg_ref[b : b + 1, :]
        negs = ids.shape[1]
        high = jnp.broadcast_to(ids >> 7, (16, negs)) == lax.broadcasted_iota(jnp.int32, (16, negs), 0)
        low = jnp.broadcast_to(ids & 127, (128, negs)) == lax.broadcasted_iota(jnp.int32, (128, negs), 0)
        table = dot_nt(jnp.where(high, 0.5, 0.0).astype(bf), jnp.where(low, 1.0, 0.0).astype(bf))
        for j in range(SLAB // 128):
            out_ref[b, 0:1, j * 128 : (j + 1) * 128] = table[j : j + 1, :]


def half_counts(neg):
    return pl.pallas_call(
        count_kernel, out_shape=jax.ShapeDtypeStruct((neg.shape[0], 1, SLAB), f32), compiler_params=params(36), name="half_counts"
    )(neg)


def whole(a):
    return pl.BlockSpec(a.shape, lambda *_: (0,) * len(a.shape))


def shape(dims, dtype):
    return jax.ShapeDtypeStruct(dims, dtype)


def columns(ids_ref, k):
    ids = [ids_ref[b, k : k + 1, :] for b in range(ids_ref.shape[0])]
    return jnp.concatenate([jnp.broadcast_to(a, (128, a.shape[1])).T for a in ids])


def hits(col, j):
    lane = lax.broadcasted_iota(jnp.int32, col.shape, 1)
    return [col == lane + (j * CHUNK + 128 * h) for h in range(2)]


def onehot(col, j):
    col = col.astype(jnp.int16)
    lane = lax.broadcasted_iota(jnp.int16, col.shape, 1)
    one, zero = jnp.ones(col.shape, bf), jnp.zeros(col.shape, bf)
    return jnp.concatenate([jnp.where(col == lane + jnp.int16(j * CHUNK + 128 * h), one, zero) for h in range(2)], axis=1)


def rows(ref, j):
    return ref[j * CHUNK : (j + 1) * CHUNK, :]


def relation_kernel(ids_ref, theta_ref, step_ref, t_ref, halves):
    @pl.when(pl.program_id(0) == 0)
    def _():
        theta = theta_ref[...] - relation_rate * step_ref[...].astype(f32)
        halves[:RELS, :] = theta.astype(bf)
        halves[RELS:, :] = (theta - theta.astype(bf).astype(f32)).astype(bf)

    rel = columns(ids_ref, 2)
    at_rel = jnp.concatenate([onehot(rel, j) for j in range(RELS // CHUNK)] * 2, axis=1)
    t_ref[...] = dot(at_rel, halves[...])


def relation_rows(ids, theta, theta_step):
    blocks, _, width = ids.shape
    return pl.pallas_call(
        relation_kernel,
        grid=(blocks // 4,),
        in_specs=[pl.BlockSpec((4,) + ids.shape[1:], lambda i: (i, 0, 0)), whole(theta), whole(theta_step)],
        out_specs=pl.BlockSpec((4 * width, W), lambda i: (i, 0)),
        out_shape=shape((blocks * width, W), f32),
        scratch_shapes=[pltpu.VMEM((2 * RELS, W), bf)],
        compiler_params=params(36),
        cost_estimate=pl.CostEstimate(flops=20_000_000_000, bytes_accessed=4_000_000, transcendentals=0),
        name="relation_rows",
    )(ids, theta, theta_step)


def grad_kernel(ids_ref, cnt_ref, t_ref, *refs):
    slabs, slab_out, theta_out = refs[:N_EDGE], refs[N_EDGE : 2 * N_EDGE], refs[2 * N_EDGE]
    left, right, all_src, all_g, all_rel, all_q, all_gs, all_gt = refs[2 * N_EDGE + 1 :]
    step = pl.program_id(0)

    @pl.when(step == 0)
    def _():
        for p in range(N_EDGE):
            left[p * PIECE : (p + 1) * PIECE, :] = slabs[p][:PIECE, :]
            right[p * PIECE : (p + 1) * PIECE, :] = slabs[p][PIECE:, :]

    src, dst, rel = (columns(ids_ref, k) for k in range(3))
    at_src = jnp.concatenate([onehot(src, j) for j in range(SLAB // CHUNK)], axis=1)
    at_rel = jnp.concatenate([onehot(rel, j) for j in range(RELS // CHUNK)], axis=1)
    t = t_ref[...]
    s = dot(at_src, left[...])
    q = (s * t).astype(bf)
    tanh = jnp.tanh(dot_nt(q * bf(0.5), right[...]))
    g = []
    for j in range(SLAB // CHUNK):
        for h, m in enumerate(hits(dst, j)):
            at = j * CHUNK + h * 128
            part = []
            for b in range(cnt_ref.shape[0]):
                e = slice(b * SPAN, (b + 1) * SPAN)
                c = cnt_ref[b, :, at : at + 128]
                part.append((jnp.where(m[e], c + 0.5, c) * tanh[e, at : at + 128] + jnp.where(m[e], c - 0.5, c)).astype(bf))
            g.append(jnp.concatenate(part))
    g = jnp.concatenate(g, axis=1)
    gq = dot(g, right[...])
    q_t = q.T
    gs = (gq * t).astype(bf).T
    gt = (gq * s).astype(bf).T
    e = pl.ds(pl.multiple_of(step * 1024, 1024), 1024)
    all_src[e, :] = at_src
    all_g[e, :] = g
    all_rel[e, :] = at_rel
    all_q[:, e] = q_t
    all_gs[:, e] = gs
    all_gt[:, e] = gt

    @pl.when(step == pl.num_programs(0) - 1)
    def _():
        for first, get in ((0, lambda j: dot(all_gs[...], all_src[:, j * CHUNK : (j + 1) * CHUNK])), (PIECE, lambda j: dot(all_q[...], all_g[:, j * CHUNK : (j + 1) * CHUNK]))):
            for j in range(SLAB // CHUNK):
                block = get(j).T.astype(bf)
                for m in range(0, CHUNK, 64):
                    p, off = divmod(j * CHUNK + m, PIECE)
                    slab_out[p][first + off : first + off + 64, :] = block[m : m + 64, :]
        for j in range(RELS // CHUNK):
            block = dot(all_gt[...], all_rel[:, j * CHUNK : (j + 1) * CHUNK]).T.astype(bf)
            for m in range(0, CHUNK, SHARE):
                theta_out[(j * CHUNK + m) // SHARE] = block[m : m + SHARE, :]


def bucket_grads(ids, counts, t, slabs):
    blocks, _, width = ids.shape
    one = lambda a: pl.BlockSpec((4,) + a.shape[1:], lambda i: (i, 0, 0))
    outs = [shape((BOTH, W), bf)] * N_EDGE + [shape((RELS // SHARE, SHARE, W), bf)]
    *g_slabs, g_theta = pl.pallas_call(
        grad_kernel,
        grid=(blocks // 4,),
        in_specs=[one(ids), one(counts), pl.BlockSpec((4 * width, W), lambda i: (i, 0))] + [whole(a) for a in slabs],
        out_specs=[whole(a) for a in outs],
        out_shape=outs,
        scratch_shapes=[
            pltpu.VMEM((SLAB, W), bf),
            pltpu.VMEM((SLAB, W), bf),
            pltpu.VMEM((2048, SLAB), bf),
            pltpu.VMEM((2048, SLAB), bf),
            pltpu.VMEM((2048, RELS), bf),
            pltpu.VMEM((W, 2048), bf),
            pltpu.VMEM((W, 2048), bf),
            pltpu.VMEM((W, 2048), bf),
        ],
        compiler_params=params(36),
        cost_estimate=pl.CostEstimate(flops=18_000_000_000, bytes_accessed=8_000_000, transcendentals=0),
        name="bucket_grads",
    )(ids, counts, t, *slabs)
    return g_slabs, g_theta


def summed(x):
    total = x[0].astype(f32)
    for k in range(1, x.shape[0]):
        total = total + x[k].astype(f32)
    return total.astype(bf)


def descend_kernel(old_ref, *refs):
    parts, left_ref, right_ref = refs[:N_EDGE], refs[N_EDGE], refs[N_EDGE + 1]
    total = parts[0][...].astype(f32)
    for part in parts[1:]:
        total = total + part[...].astype(f32)
    new = (old_ref[...].astype(f32) - learn_rate * total).astype(bf)
    left_ref[...] = new[:PIECE]
    right_ref[...] = new[PIECE:]


def descend(parts, old):
    out = shape((PIECE, W), bf)
    return pl.pallas_call(descend_kernel, out_shape=[out, out], compiler_params=params(36), name="descend")(old, *parts)


def theta_kernel(old_ref, step_ref, new_ref):
    new_ref[...] = old_ref[...] - relation_rate * step_ref[...].astype(f32)


def stepped(theta, theta_step):
    return pl.pallas_call(
        theta_kernel, out_shape=shape(theta.shape, f32), compiler_params=params(36), name="stepped"
    )(theta, theta_step)


def exchange(x, axes):
    return lax.all_to_all(x, axes, 0, 0)


def to_all(x, axes):
    n = lax.axis_size(axes)
    return exchange(jnp.broadcast_to(x[None], (n,) + x.shape), axes)


def along_edge(x, k):
    n = lax.axis_size(EDGE)
    return lax.ppermute(x, EDGE, [(i, (i + k) % n) for i in range(n)])


def gathered(x):
    got = {p: along_edge(x, p) for p in SHIFTS}
    return [x] + [got[p] for p in range(1, N_EDGE)]


def returned(pieces):
    got = {p: along_edge(pieces[p], -p) for p in SHIFTS}
    return [pieces[0]] + [got[p] for p in range(1, N_EDGE)]


def next_group(x):
    n = lax.axis_size(BUCKET)
    return lax.ppermute(x, BUCKET, [(i, (i + 1) % n) for i in range(n)])


def body(left_slab, right_slab, relation, src_ids, dst_ids, rel_ids, neg_ids, edge_counts):
    me = lax.axis_index(EDGE)
    blocks = neg_ids.shape[2]
    width = src_ids.shape[2] // blocks

    def local(ids):
        owner = ids // PIECE
        return lax.rem(me - owner + N_EDGE, N_EDGE) * PIECE + (ids - owner * PIECE)

    own = jnp.concatenate([left_slab, right_slab])
    slabs = gathered(own)
    slot = me * blocks * width + jnp.arange(blocks * width)
    live = slot[None] < edge_counts
    src = jnp.where(live, local(src_ids[:, 0]), -1)
    rel = jnp.where(live, rel_ids[:, 0], -1)
    ids = jnp.stack([a.reshape(ROUNDS, blocks, width) for a in (src, local(dst_ids[:, 0]), rel)] + [jnp.zeros((ROUNDS, blocks, width), jnp.int32)] * 5, 2)
    counts = half_counts(local(neg_ids[:, 0]).reshape(ROUNDS * blocks, -1)).reshape(ROUNDS, blocks, 1, SLAB)
    theta = relation.reshape(RELS // SHARE, SHARE, W)
    theta_step = jnp.zeros(theta.shape, bf)
    for rnd in range(ROUNDS):
        t = relation_rows(ids[rnd], theta.reshape(RELS, W), theta_step.reshape(RELS, W))
        g_slabs, g_theta = bucket_grads(ids[rnd], counts[rnd], t, slabs)
        if rnd > 0:
            theta = stepped(theta, theta_step)
        parts = returned(g_slabs)
        g_theta = summed(to_all(summed(exchange(g_theta, PLANE)), "z"))
        if rnd + 1 == ROUNDS:
            parts, g_theta = lax.optimization_barrier((parts, g_theta))
        theta_step = to_all(g_theta, PLANE)
        left, right = descend(parts, own)
        if rnd + 1 < ROUNDS:
            own = jnp.concatenate([left, next_group(right)])
            slabs = gathered(own)
    return (left, right, stepped(theta, theta_step).reshape(RELS, W))


def solution(mesh):
    fine = Mesh(mesh.devices.reshape(8, 2, 2, 4, 2), BUCKET + EDGE)
    rows = P(BUCKET + EDGE, None)
    placed = (
        rows,
        rows,
        P(),
        P(None, BUCKET, EDGE),
        P(None, BUCKET, EDGE),
        P(None, BUCKET, EDGE),
        P(None, BUCKET, EDGE, None),
        P(None, BUCKET),
    )
    return jax.shard_map(
        body,
        mesh=fine,
        in_specs=placed,
        out_specs=(rows, rows, P()),
        check_vma=False,
    )
```

```python
import jax
import jax.numpy as jnp
from jax import lax
from jax.experimental import pallas as pl
from jax.experimental.pallas import tpu as pltpu
from jax.sharding import Mesh
from jax.sharding import PartitionSpec as P

ROUNDS = 2
N_EDGE = 8
SLAB = 1536
RELS = 1024
W = 256
BOTH = 2 * (SLAB // N_EDGE)
PIECE = SLAB // N_EDGE
SHARE = 32
SHIFTS = (4, 3, 5, 2, 6, 7, 1)
CHUNK = 256
SPAN = 256

learn_rate = 0.05
relation_rate = 0.05

EDGE = ("x", "y_lo")
BUCKET = ("z", "y_hi", "core")
PLANE = EDGE + ("y_hi", "core")

bf = jnp.bfloat16
f32 = jnp.float32


def dot(a, b):
    return jnp.dot(a, b, preferred_element_type=f32)


def dot_nt(a, b):
    return lax.dot_general(a, b, (((1,), (1,)), ((), ())), preferred_element_type=f32)


def params(mib):
    return pltpu.CompilerParams(vmem_limit_bytes=mib << 20)


def count_kernel(neg_ref, out_ref):
    for b in range(neg_ref.shape[0]):
        ids = neg_ref[b : b + 1, :]
        negs = ids.shape[1]
        high = jnp.broadcast_to(ids >> 7, (16, negs)) == lax.broadcasted_iota(jnp.int32, (16, negs), 0)
        low = jnp.broadcast_to(ids & 127, (128, negs)) == lax.broadcasted_iota(jnp.int32, (128, negs), 0)
        table = dot_nt(jnp.where(high, 0.5, 0.0).astype(bf), jnp.where(low, 1.0, 0.0).astype(bf))
        for j in range(SLAB // 128):
            out_ref[b, 0:1, j * 128 : (j + 1) * 128] = table[j : j + 1, :]


def half_counts(neg):
    return pl.pallas_call(
        count_kernel, out_shape=jax.ShapeDtypeStruct((neg.shape[0], 1, SLAB), f32), compiler_params=params(36), name="half_counts"
    )(neg)


def whole(a):
    return pl.BlockSpec(a.shape, lambda *_: (0,) * len(a.shape))


def shape(dims, dtype):
    return jax.ShapeDtypeStruct(dims, dtype)


def columns(ids_ref, k):
    ids = [ids_ref[b, k : k + 1, :] for b in range(ids_ref.shape[0])]
    return jnp.concatenate([jnp.broadcast_to(a, (128, a.shape[1])).T for a in ids])


def hits(col, j):
    lane = lax.broadcasted_iota(jnp.int32, col.shape, 1)
    return [col == lane + (j * CHUNK + 128 * h) for h in range(2)]


def onehot(col, j):
    col = col.astype(jnp.int16)
    lane = lax.broadcasted_iota(jnp.int16, col.shape, 1)
    one, zero = jnp.ones(col.shape, bf), jnp.zeros(col.shape, bf)
    return jnp.concatenate([jnp.where(col == lane + jnp.int16(j * CHUNK + 128 * h), one, zero) for h in range(2)], axis=1)


def rows(ref, j):
    return ref[j * CHUNK : (j + 1) * CHUNK, :]


def relation_kernel(ids_ref, theta_ref, step_ref, t_ref, halves):
    @pl.when(pl.program_id(0) == 0)
    def _():
        theta = theta_ref[...] - relation_rate * step_ref[...].astype(f32)
        halves[:RELS, :] = theta.astype(bf)
        halves[RELS:, :] = (theta - theta.astype(bf).astype(f32)).astype(bf)

    rel = columns(ids_ref, 2)
    at_rel = jnp.concatenate([onehot(rel, j) for j in range(RELS // CHUNK)] * 2, axis=1)
    t_ref[...] = dot(at_rel, halves[...])


def relation_rows(ids, theta, theta_step):
    blocks, _, width = ids.shape
    return pl.pallas_call(
        relation_kernel,
        grid=(blocks // 4,),
        in_specs=[pl.BlockSpec((4,) + ids.shape[1:], lambda i: (i, 0, 0)), whole(theta), whole(theta_step)],
        out_specs=pl.BlockSpec((4 * width, W), lambda i: (i, 0)),
        out_shape=shape((blocks * width, W), f32),
        scratch_shapes=[pltpu.VMEM((2 * RELS, W), bf)],
        compiler_params=params(36),
        cost_estimate=pl.CostEstimate(flops=20_000_000_000, bytes_accessed=4_000_000, transcendentals=0),
        name="relation_rows",
    )(ids, theta, theta_step)


def grad_kernel(ids_ref, cnt_ref, t_ref, *refs):
    slabs, slab_out, theta_out = refs[:N_EDGE], refs[N_EDGE : 2 * N_EDGE], refs[2 * N_EDGE]
    left, right, all_src, all_g, all_rel, all_q, all_gs, all_gt = refs[2 * N_EDGE + 1 :]
    step = pl.program_id(0)

    @pl.when(step == 0)
    def _():
        for p in range(N_EDGE):
            left[p * PIECE : (p + 1) * PIECE, :] = slabs[p][:PIECE, :]
            right[p * PIECE : (p + 1) * PIECE, :] = slabs[p][PIECE:, :]

    src, dst, rel = (columns(ids_ref, k) for k in range(3))
    at_src = jnp.concatenate([onehot(src, j) for j in range(SLAB // CHUNK)], axis=1)
    at_rel = jnp.concatenate([onehot(rel, j) for j in range(RELS // CHUNK)], axis=1)
    t = t_ref[...]
    s = dot(at_src, left[...])
    q = (s * t).astype(bf)
    tanh = jnp.tanh(dot_nt(q * bf(0.5), right[...]))
    g = []
    for j in range(SLAB // CHUNK):
        for h, m in enumerate(hits(dst, j)):
            at = j * CHUNK + h * 128
            part = []
            for b in range(cnt_ref.shape[0]):
                e = slice(b * SPAN, (b + 1) * SPAN)
                c = cnt_ref[b, :, at : at + 128]
                part.append((jnp.where(m[e], c + 0.5, c) * tanh[e, at : at + 128] + jnp.where(m[e], c - 0.5, c)).astype(bf))
            g.append(jnp.concatenate(part))
    g = jnp.concatenate(g, axis=1)
    gq = dot(g, right[...])
    q_t = q.T
    gs = (gq * t).astype(bf).T
    gt = (gq * s).astype(bf).T
    e = pl.ds(pl.multiple_of(step * 1024, 1024), 1024)
    all_src[e, :] = at_src
    all_g[e, :] = g
    all_rel[e, :] = at_rel
    all_q[:, e] = q_t
    all_gs[:, e] = gs
    all_gt[:, e] = gt

    @pl.when(step == pl.num_programs(0) - 1)
    def _():
        for first, get in ((0, lambda j: dot(all_gs[...], all_src[:, j * CHUNK : (j + 1) * CHUNK])), (PIECE, lambda j: dot(all_q[...], all_g[:, j * CHUNK : (j + 1) * CHUNK]))):
            for j in range(SLAB // CHUNK):
                block = get(j).T.astype(bf)
                for m in range(0, CHUNK, 64):
                    p, off = divmod(j * CHUNK + m, PIECE)
                    slab_out[p][first + off : first + off + 64, :] = block[m : m + 64, :]
        for j in range(RELS // CHUNK):
            block = dot(all_gt[...], all_rel[:, j * CHUNK : (j + 1) * CHUNK]).T.astype(bf)
            for m in range(0, CHUNK, SHARE):
                theta_out[(j * CHUNK + m) // SHARE] = block[m : m + SHARE, :]


def bucket_grads(ids, counts, t, slabs):
    blocks, _, width = ids.shape
    one = lambda a: pl.BlockSpec((4,) + a.shape[1:], lambda i: (i, 0, 0))
    outs = [shape((BOTH, W), bf)] * N_EDGE + [shape((RELS // SHARE, SHARE, W), bf)]
    *g_slabs, g_theta = pl.pallas_call(
        grad_kernel,
        grid=(blocks // 4,),
        in_specs=[one(ids), one(counts), pl.BlockSpec((4 * width, W), lambda i: (i, 0))] + [whole(a) for a in slabs],
        out_specs=[whole(a) for a in outs],
        out_shape=outs,
        scratch_shapes=[
            pltpu.VMEM((SLAB, W), bf),
            pltpu.VMEM((SLAB, W), bf),
            pltpu.VMEM((2048, SLAB), bf),
            pltpu.VMEM((2048, SLAB), bf),
            pltpu.VMEM((2048, RELS), bf),
            pltpu.VMEM((W, 2048), bf),
            pltpu.VMEM((W, 2048), bf),
            pltpu.VMEM((W, 2048), bf),
        ],
        compiler_params=params(36),
        cost_estimate=pl.CostEstimate(flops=18_000_000_000, bytes_accessed=8_000_000, transcendentals=0),
        name="bucket_grads",
    )(ids, counts, t, *slabs)
    return g_slabs, g_theta


def summed(x, copies):
    def kernel(x_ref, out_ref):
        total = x_ref[0].astype(f32)
        for k in range(1, x.shape[0]):
            total = total + x_ref[k].astype(f32)
        total = total.astype(bf)
        for k in range(copies):
            out_ref[k] = total

    return pl.pallas_call(
        kernel, out_shape=shape((copies,) + x.shape[1:], bf), compiler_params=params(36), name="summed"
    )(x)


def joined_kernel(top_ref, bottom_ref, out_ref):
    out_ref[:PIECE, :] = top_ref[...]
    out_ref[PIECE:, :] = bottom_ref[...]


def joined(top, bottom):
    return pl.pallas_call(
        joined_kernel, out_shape=shape((BOTH, W), bf), compiler_params=params(36), name="joined"
    )(top, bottom)


def descend_kernel(old_ref, *refs):
    parts, left_ref, right_ref = refs[:N_EDGE], refs[N_EDGE], refs[N_EDGE + 1]
    total = parts[0][...].astype(f32)
    for part in parts[1:]:
        total = total + part[...].astype(f32)
    new = (old_ref[...].astype(f32) - learn_rate * total).astype(bf)
    left_ref[...] = new[:PIECE]
    right_ref[...] = new[PIECE:]


def descend(parts, old):
    out = shape((PIECE, W), bf)
    return pl.pallas_call(descend_kernel, out_shape=[out, out], compiler_params=params(36), name="descend")(old, *parts)


def theta_kernel(old_ref, step_ref, new_ref):
    new_ref[...] = old_ref[...] - relation_rate * step_ref[...].astype(f32)


def stepped(theta, theta_step):
    return pl.pallas_call(
        theta_kernel, out_shape=shape(theta.shape, f32), compiler_params=params(36), name="stepped"
    )(theta, theta_step)


def exchange(x, axes):
    return lax.all_to_all(x, axes, 0, 0)


def along_edge(x, k):
    n = lax.axis_size(EDGE)
    return lax.ppermute(x, EDGE, [(i, (i + k) % n) for i in range(n)])


def gathered(x):
    got = {p: along_edge(x, p) for p in SHIFTS}
    return [x] + [got[p] for p in range(1, N_EDGE)]


def returned(pieces):
    got = {p: along_edge(pieces[p], -p) for p in SHIFTS}
    return [pieces[0]] + [got[p] for p in range(1, N_EDGE)]


def next_group(x):
    n = lax.axis_size(BUCKET)
    return lax.ppermute(x, BUCKET, [(i, (i + 1) % n) for i in range(n)])


def body(left_slab, right_slab, relation, src_ids, dst_ids, rel_ids, neg_ids, edge_counts):
    me = lax.axis_index(EDGE)
    blocks = neg_ids.shape[2]
    width = src_ids.shape[2] // blocks

    def local(ids):
        owner = ids // PIECE
        return lax.rem(me - owner + N_EDGE, N_EDGE) * PIECE + (ids - owner * PIECE)

    own = joined(left_slab, right_slab)
    slabs = gathered(own)
    slot = me * blocks * width + jnp.arange(blocks * width)
    live = slot[None] < edge_counts
    src = jnp.where(live, local(src_ids[:, 0]), -1)
    rel = jnp.where(live, rel_ids[:, 0], -1)
    ids = jnp.stack([a.reshape(ROUNDS, blocks, width) for a in (src, local(dst_ids[:, 0]), rel)] + [jnp.zeros((ROUNDS, blocks, width), jnp.int32)] * 5, 2)
    counts = half_counts(local(neg_ids[:, 0]).reshape(ROUNDS * blocks, -1)).reshape(ROUNDS, blocks, 1, SLAB)
    theta = relation.reshape(RELS // SHARE, SHARE, W)
    theta_step = jnp.zeros(theta.shape, bf)
    for rnd in range(ROUNDS):
        t = relation_rows(ids[rnd], theta.reshape(RELS, W), theta_step.reshape(RELS, W))
        g_slabs, g_theta = bucket_grads(ids[rnd], counts[rnd], t, slabs)
        if rnd > 0:
            theta = stepped(theta, theta_step)
        parts = returned(g_slabs)
        g_theta = summed(exchange(g_theta, PLANE), lax.axis_size("z"))
        g_theta = summed(exchange(g_theta, "z"), lax.axis_size(PLANE))
        if rnd + 1 == ROUNDS:
            parts, g_theta = lax.optimization_barrier((parts, g_theta))
        theta_step = exchange(g_theta, PLANE)
        left, right = descend(parts, own)
        if rnd + 1 < ROUNDS:
            own = jnp.concatenate([left, next_group(right)])
            slabs = gathered(own)
    return (left, right, stepped(theta, theta_step).reshape(RELS, W))


def solution(mesh):
    fine = Mesh(mesh.devices.reshape(8, 2, 2, 4, 2), BUCKET + EDGE)
    rows = P(BUCKET + EDGE, None)
    placed = (
        rows,
        rows,
        P(),
        P(None, BUCKET, EDGE),
        P(None, BUCKET, EDGE),
        P(None, BUCKET, EDGE),
        P(None, BUCKET, EDGE, None),
        P(None, BUCKET),
    )
    return jax.shard_map(
        body,
        mesh=fine,
        in_specs=placed,
        out_specs=(rows, rows, P()),
        check_vma=False,
    )
```

```python
import jax
import jax.numpy as jnp
from jax import lax
from jax.experimental import pallas as pl
from jax.experimental.pallas import tpu as pltpu
from jax.sharding import Mesh
from jax.sharding import PartitionSpec as P

ROUNDS = 2
N_EDGE = 8
SLAB = 1536
RELS = 1024
W = 256
BOTH = 2 * (SLAB // N_EDGE)
PIECE = SLAB // N_EDGE
SHARE = 32
SHIFTS = (4, 3, 5, 2, 6, 7, 1)
CHUNK = 256
SPAN = 256

learn_rate = 0.05
relation_rate = 0.05

EDGE = ("x", "y_lo")
BUCKET = ("z", "y_hi", "core")
PLANE = EDGE + ("y_hi", "core")

bf = jnp.bfloat16
f32 = jnp.float32


def dot(a, b):
    return jnp.dot(a, b, preferred_element_type=f32)


def dot_nt(a, b):
    return lax.dot_general(a, b, (((1,), (1,)), ((), ())), preferred_element_type=f32)


def params(mib):
    return pltpu.CompilerParams(vmem_limit_bytes=mib << 20)


def count_kernel(neg_ref, out_ref):
    for b in range(neg_ref.shape[0]):
        ids = neg_ref[b : b + 1, :]
        negs = ids.shape[1]
        high = jnp.broadcast_to(ids >> 7, (16, negs)) == lax.broadcasted_iota(jnp.int32, (16, negs), 0)
        low = jnp.broadcast_to(ids & 127, (128, negs)) == lax.broadcasted_iota(jnp.int32, (128, negs), 0)
        table = dot_nt(jnp.where(high, 0.5, 0.0).astype(bf), jnp.where(low, 1.0, 0.0).astype(bf))
        for j in range(SLAB // 128):
            out_ref[b, 0:1, j * 128 : (j + 1) * 128] = table[j : j + 1, :]


def half_counts(neg):
    return pl.pallas_call(
        count_kernel, out_shape=jax.ShapeDtypeStruct((neg.shape[0], 1, SLAB), f32), compiler_params=params(36), name="half_counts"
    )(neg)


def whole(a):
    return pl.BlockSpec(a.shape, lambda *_: (0,) * len(a.shape))


def shape(dims, dtype):
    return jax.ShapeDtypeStruct(dims, dtype)


def columns(ids_ref, k):
    ids = [ids_ref[b, k : k + 1, :] for b in range(ids_ref.shape[0])]
    return jnp.concatenate([jnp.broadcast_to(a, (128, a.shape[1])).T for a in ids])


def hits(col, j):
    lane = lax.broadcasted_iota(jnp.int32, col.shape, 1)
    return [col == lane + (j * CHUNK + 128 * h) for h in range(2)]


def onehot(col, j):
    col = col.astype(jnp.int16)
    lane = lax.broadcasted_iota(jnp.int16, col.shape, 1)
    one, zero = jnp.ones(col.shape, bf), jnp.zeros(col.shape, bf)
    return jnp.concatenate([jnp.where(col == lane + jnp.int16(j * CHUNK + 128 * h), one, zero) for h in range(2)], axis=1)


def rows(ref, j):
    return ref[j * CHUNK : (j + 1) * CHUNK, :]


def relation_kernel(ids_ref, theta_ref, step_ref, t_ref, halves):
    @pl.when(pl.program_id(0) == 0)
    def _():
        theta = theta_ref[...] - relation_rate * step_ref[...].astype(f32)
        halves[:RELS, :] = theta.astype(bf)
        halves[RELS:, :] = (theta - theta.astype(bf).astype(f32)).astype(bf)

    rel = columns(ids_ref, 2)
    at_rel = jnp.concatenate([onehot(rel, j) for j in range(RELS // CHUNK)] * 2, axis=1)
    t_ref[...] = dot(at_rel, halves[...])


def relation_rows(ids, theta, theta_step):
    blocks, _, width = ids.shape
    return pl.pallas_call(
        relation_kernel,
        grid=(blocks // 4,),
        in_specs=[pl.BlockSpec((4,) + ids.shape[1:], lambda i: (i, 0, 0)), whole(theta), whole(theta_step)],
        out_specs=pl.BlockSpec((4 * width, W), lambda i: (i, 0)),
        out_shape=shape((blocks * width, W), f32),
        scratch_shapes=[pltpu.VMEM((2 * RELS, W), bf)],
        compiler_params=params(36),
        cost_estimate=pl.CostEstimate(flops=20_000_000_000, bytes_accessed=4_000_000, transcendentals=0),
        name="relation_rows",
    )(ids, theta, theta_step)


def grad_kernel(ids_ref, cnt_ref, t_ref, *refs):
    slabs, slab_out, theta_out = refs[:N_EDGE], refs[N_EDGE : 2 * N_EDGE], refs[2 * N_EDGE]
    left, right, all_src, all_g, all_rel, all_q, all_gs, all_gt = refs[2 * N_EDGE + 1 :]
    step = pl.program_id(0)

    @pl.when(step == 0)
    def _():
        for p in range(N_EDGE):
            left[p * PIECE : (p + 1) * PIECE, :] = slabs[p][:PIECE, :]
            right[p * PIECE : (p + 1) * PIECE, :] = slabs[p][PIECE:, :]

    src, dst, rel = (columns(ids_ref, k) for k in range(3))
    at_src = jnp.concatenate([onehot(src, j) for j in range(SLAB // CHUNK)], axis=1)
    at_rel = jnp.concatenate([onehot(rel, j) for j in range(RELS // CHUNK)], axis=1)
    t = t_ref[...]
    s = dot(at_src, left[...])
    q = (s * t).astype(bf)
    tanh = jnp.tanh(dot_nt(q * bf(0.5), right[...]))
    g = []
    for j in range(SLAB // CHUNK):
        for h, m in enumerate(hits(dst, j)):
            at = j * CHUNK + h * 128
            part = []
            for b in range(cnt_ref.shape[0]):
                e = slice(b * SPAN, (b + 1) * SPAN)
                c = cnt_ref[b, :, at : at + 128]
                part.append((jnp.where(m[e], c + 0.5, c) * tanh[e, at : at + 128] + jnp.where(m[e], c - 0.5, c)).astype(bf))
            g.append(jnp.concatenate(part))
    g = jnp.concatenate(g, axis=1)
    gq = dot(g, right[...])
    q_t = q.T
    gs = (gq * t).astype(bf).T
    gt = (gq * s).astype(bf).T
    e = pl.ds(pl.multiple_of(step * 1024, 1024), 1024)
    all_src[e, :] = at_src
    all_g[e, :] = g
    all_rel[e, :] = at_rel
    all_q[:, e] = q_t
    all_gs[:, e] = gs
    all_gt[:, e] = gt

    @pl.when(step == pl.num_programs(0) - 1)
    def _():
        for first, get in ((0, lambda j: dot(all_gs[...], all_src[:, j * CHUNK : (j + 1) * CHUNK])), (PIECE, lambda j: dot(all_q[...], all_g[:, j * CHUNK : (j + 1) * CHUNK]))):
            for j in range(SLAB // CHUNK):
                block = get(j).T.astype(bf)
                for m in range(0, CHUNK, 64):
                    p, off = divmod(j * CHUNK + m, PIECE)
                    slab_out[p][first + off : first + off + 64, :] = block[m : m + 64, :]
        for j in range(RELS // CHUNK):
            block = dot(all_gt[...], all_rel[:, j * CHUNK : (j + 1) * CHUNK]).T.astype(bf)
            for m in range(0, CHUNK, SHARE):
                theta_out[(j * CHUNK + m) // SHARE] = block[m : m + SHARE, :]


def bucket_grads(ids, counts, t, slabs):
    blocks, _, width = ids.shape
    one = lambda a: pl.BlockSpec((4,) + a.shape[1:], lambda i: (i, 0, 0))
    outs = [shape((BOTH, W), bf)] * N_EDGE + [shape((RELS // SHARE, SHARE, W), bf)]
    *g_slabs, g_theta = pl.pallas_call(
        grad_kernel,
        grid=(blocks // 4,),
        in_specs=[one(ids), one(counts), pl.BlockSpec((4 * width, W), lambda i: (i, 0))] + [whole(a) for a in slabs],
        out_specs=[whole(a) for a in outs],
        out_shape=outs,
        scratch_shapes=[
            pltpu.VMEM((SLAB, W), bf),
            pltpu.VMEM((SLAB, W), bf),
            pltpu.VMEM((2048, SLAB), bf),
            pltpu.VMEM((2048, SLAB), bf),
            pltpu.VMEM((2048, RELS), bf),
            pltpu.VMEM((W, 2048), bf),
            pltpu.VMEM((W, 2048), bf),
            pltpu.VMEM((W, 2048), bf),
        ],
        compiler_params=params(36),
        cost_estimate=pl.CostEstimate(flops=18_000_000_000, bytes_accessed=8_000_000, transcendentals=0),
        name="bucket_grads",
    )(ids, counts, t, *slabs)
    return g_slabs, g_theta


def summed(x, copies):
    def kernel(x_ref, out_ref):
        total = x_ref[0].astype(f32)
        for k in range(1, x.shape[0]):
            total = total + x_ref[k].astype(f32)
        total = total.astype(bf)
        for k in range(copies):
            out_ref[k] = total

    return pl.pallas_call(
        kernel, out_shape=shape((copies,) + x.shape[1:], bf), compiler_params=params(36), name="summed"
    )(x)


def joined_kernel(top_ref, bottom_ref, out_ref):
    out_ref[:PIECE, :] = top_ref[...]
    out_ref[PIECE:, :] = bottom_ref[...]


def joined(top, bottom):
    return pl.pallas_call(
        joined_kernel, out_shape=shape((BOTH, W), bf), compiler_params=params(36), name="joined"
    )(top, bottom)


def descend_kernel(old_ref, *refs):
    parts, left_ref, right_ref = refs[:N_EDGE], refs[N_EDGE], refs[N_EDGE + 1]
    total = parts[0][...].astype(f32)
    for part in parts[1:]:
        total = total + part[...].astype(f32)
    new = (old_ref[...].astype(f32) - learn_rate * total).astype(bf)
    left_ref[...] = new[:PIECE]
    right_ref[...] = new[PIECE:]


def descend(parts, old):
    out = shape((PIECE, W), bf)
    return pl.pallas_call(descend_kernel, out_shape=[out, out], compiler_params=params(36), name="descend")(old, *parts)


def theta_kernel(old_ref, step_ref, new_ref):
    new_ref[...] = old_ref[...] - relation_rate * step_ref[...].astype(f32)


def stepped(theta, theta_step):
    return pl.pallas_call(
        theta_kernel, out_shape=shape(theta.shape, f32), compiler_params=params(36), name="stepped"
    )(theta, theta_step)


def exchange(x, axes):
    return lax.all_to_all(x, axes, 0, 0)


def along_edge(x, k):
    n = lax.axis_size(EDGE)
    return lax.ppermute(x, EDGE, [(i, (i + k) % n) for i in range(n)])


def gathered(x):
    got = {p: along_edge(x, p) for p in SHIFTS}
    return [x] + [got[p] for p in range(1, N_EDGE)]


def returned(pieces):
    got = {p: along_edge(pieces[p], -p) for p in SHIFTS}
    return [pieces[0]] + [got[p] for p in range(1, N_EDGE)]


def next_group(x):
    n = lax.axis_size(BUCKET)
    return lax.ppermute(x, BUCKET, [(i, (i + 1) % n) for i in range(n)])


def body(left_slab, right_slab, relation, src_ids, dst_ids, rel_ids, neg_ids, edge_counts):
    me = lax.axis_index(EDGE)
    blocks = neg_ids.shape[2]
    width = src_ids.shape[2] // blocks

    def local(ids):
        owner = ids // PIECE
        return lax.rem(me - owner + N_EDGE, N_EDGE) * PIECE + (ids - owner * PIECE)

    own = joined(left_slab, right_slab)
    slabs = gathered(own)
    slot = me * blocks * width + jnp.arange(blocks * width)
    live = slot[None] < edge_counts
    src = jnp.where(live, local(src_ids[:, 0]), -1)
    rel = jnp.where(live, rel_ids[:, 0], -1)
    ids = jnp.stack([a.reshape(ROUNDS, blocks, width) for a in (src, local(dst_ids[:, 0]), rel)] + [jnp.zeros((ROUNDS, blocks, width), jnp.int32)] * 5, 2)
    counts = half_counts(local(neg_ids[:, 0]).reshape(ROUNDS * blocks, -1)).reshape(ROUNDS, blocks, 1, SLAB)
    theta = relation.reshape(RELS // SHARE, SHARE, W)
    theta_step = jnp.zeros(theta.shape, bf)
    for rnd in range(ROUNDS):
        t = relation_rows(ids[rnd], theta.reshape(RELS, W), theta_step.reshape(RELS, W))
        g_slabs, g_theta = bucket_grads(ids[rnd], counts[rnd], t, slabs)
        if rnd > 0:
            theta = stepped(theta, theta_step)
        parts = returned(g_slabs)
        g_theta = summed(exchange(g_theta, PLANE), lax.axis_size("z"))
        g_theta = summed(exchange(g_theta, "z"), lax.axis_size(PLANE))
        if rnd + 1 == ROUNDS:
            parts, g_theta = lax.optimization_barrier((parts, g_theta))
        theta_step = exchange(g_theta, PLANE)
        left, right = descend(parts, own)
        if rnd + 1 < ROUNDS:
            own = joined(left, next_group(right))
            slabs = gathered(own)
    return (left, right, stepped(theta, theta_step).reshape(RELS, W))


def solution(mesh):
    fine = Mesh(mesh.devices.reshape(8, 2, 2, 4, 2), BUCKET + EDGE)
    rows = P(BUCKET + EDGE, None)
    placed = (
        rows,
        rows,
        P(),
        P(None, BUCKET, EDGE),
        P(None, BUCKET, EDGE),
        P(None, BUCKET, EDGE),
        P(None, BUCKET, EDGE, None),
        P(None, BUCKET),
    )
    return jax.shard_map(
        body,
        mesh=fine,
        in_specs=placed,
        out_specs=(rows, rows, P()),
        check_vma=False,
    )
```
